256 devices in a mesh: poke: 32 (over z_hi, x, y), sensor: 8 (over z_lo, core).
Axes of the slice: x: 4, y: 4, z: 8 (z_hi: 2, z_lo: 4; z = z_hi * 4 + z_lo), core: 2. Of those that a mesh axis runs over, the one named last changes fastest.
Arguments:
- push_slopes: bfloat16 [8192, 6, 8192], P('poke', None, 'sensor'), may hold values from -6 to 6
- pull_slopes: bfloat16 [8192, 6, 8192], P('poke', None, 'sensor'), may hold values from -6 to 6
- pattern_order: int32 [256], replicated, may hold values from 0 to 255, each once
- star_map: int32 [6, 8192], P(None, 'sensor'), may hold values from 0 to 8191, as said below
Outputs:
- gram_matrix: float32 [8192, 8192], P('poke', 'sensor')
The draws below stay inside these ranges and needn't reach their ends.
Inputs may be any that keep to these rules, and one draw needn't show every extreme that they name: `pattern_order`: a permutation of 0 to 255. `star_map`: each row is a permutation of 0 to 8191 that keeps every index within its aligned block of 1024 slopes.
All inputs are finite; a program needn't handle non-finite values.
Results may differ from the reference program's by a relative error of at most 0.0042.
Values may be sent and summed in bfloat16 or wider, within the bound.
A program may use at most 128 MiB of HBM per device.

```python
import math
import jax
import jax.numpy as jnp
from jax import lax

FRAMES = 8192
STARS = 6
SL_DEV = 1024
SLOPES = 8192
FB = 256
N_POKE = 32


def draw_star_map(key, part):
    key = jax.random.fold_in(key, 7)
    block_total = SLOPES // SL_DEV
    key_list = jax.random.split(key, STARS * block_total)
    shuffled = jax.vmap(lambda single: jax.random.permutation(single, SL_DEV))(key_list)
    shuffled = shuffled.reshape(STARS, block_total, SL_DEV).astype(jnp.int32)
    offsets = (jnp.arange(block_total, dtype=jnp.int32) * SL_DEV)[None, :, None]
    return (shuffled + offsets).reshape(STARS, SLOPES)


def steps_of(stream_key, dims, shards, smallest, high):
    def one(axis_at, parts):
        steps = jax.random.uniform(jax.random.fold_in(jax.random.fold_in(stream_key, 6), axis_at), (parts,), jnp.float32, smallest / len(shards), high / len(shards))
        return jnp.repeat(jnp.exp(steps), dims[axis_at] // parts).reshape((-1,) + (1,) * (len(dims) - axis_at - 1))

    factor_of = one(*shards[0])
    for cut in shards[1:]:
        factor_of = factor_of * one(*cut)
    return factor_of


def bell_draw(rng, dims, spread, most, cuts=(), held_as=jnp.bfloat16):
    level = steps_of(rng, dims, cuts, -0.22, 0.18) if cuts else 1.0
    result = jax.random.normal(rng, dims, jnp.float32) * spread * level
    return jnp.minimum(jnp.maximum(result, -most), most).astype(held_as)


def setup_inputs(seed: int = 0) -> dict:
    seeds = jax.random.split(jax.random.key(seed), 5)
    return {
        "push_slopes": bell_draw(seeds[0], (FRAMES, STARS, SLOPES), 1.0, 6.0, ((0, 32), (2, 8))),
        "pull_slopes": bell_draw(seeds[1], (FRAMES, STARS, SLOPES), 1.0, 6.0, ((0, 32), (2, 8))),
        "pattern_order": jax.random.permutation(seeds[2], FB).astype(jnp.int32),
        "star_map": draw_star_map(jax.random.fold_in(seeds[4], 71), 0),
    }


def sign_table(first_index, second_index, bit_count):
    masked = jnp.bitwise_and(first_index[:, None], second_index[None, :])
    parity = jnp.zeros(masked.shape, jnp.int32)
    for shift_bits in range(bit_count):
        parity = parity + jnp.bitwise_and(jnp.right_shift(masked, shift_bits), 1)
    return (1 - 2 * (parity % 2)).astype(jnp.float32)

def reference(push_slopes, pull_slopes, pattern_order, star_map):
    accumulated = jnp.zeros((FRAMES, SLOPES), jnp.float32)
    for star_index in range(STARS):
        difference = (push_slopes[:, star_index, :].astype(jnp.float32) - pull_slopes[:, star_index, :].astype(jnp.float32)).astype(jnp.bfloat16)
        accumulated = accumulated + jnp.take(difference, star_map[star_index], axis=1).astype(jnp.float32)
    averaged = accumulated / STARS
    sign_local = sign_table(jnp.arange(FB, dtype=jnp.int32), pattern_order.astype(jnp.int32), FB.bit_length())
    across_index = jnp.arange(N_POKE, dtype=jnp.int32)
    sign_across = sign_table(across_index, across_index, N_POKE.bit_length())
    blocks = averaged.reshape(N_POKE, FB, SLOPES)
    transformed = jnp.einsum('hb,abs->ahs', sign_local, blocks, precision=lax.Precision.HIGHEST)
    mixed_modes = jnp.einsum('la,ahs->hls', sign_across, transformed, precision=lax.Precision.HIGHEST)
    demodulated = (mixed_modes.reshape(FRAMES, SLOPES) / math.sqrt(FRAMES)).astype(jnp.bfloat16)
    gram_matrix = jnp.dot(demodulated, demodulated.T, preferred_element_type=jnp.float32)
    return gram_matrix / math.sqrt(SLOPES)
```

```python
import functools
import math

import jax
import jax.numpy as jnp
from jax import lax
from jax.experimental import pallas as pl
from jax.experimental.pallas import tpu as pltpu
from jax.sharding import PartitionSpec as P

MESH = pl.DeviceIdType.MESH
STARS, FRAMES, SLOPES = 6, 256, 1024
HALF = SLOPES // 2
ROWS = 512
KEPT = 5
F32, BF16 = jnp.float32, jnp.bfloat16


def parity(bits):
    for shift in (4, 2, 1):
        bits = bits ^ (bits >> shift)
    return bits & 1


def star_kernel(push_ref, pull_ref, order_ref, map_ref, t_ref, total):
    star = pl.program_id(0)
    difference = (push_ref[0].astype(F32) - pull_ref[0].astype(F32)).astype(BF16)
    index = map_ref[pl.ds(star, 1), :] % SLOPES
    hot = (lax.broadcasted_iota(jnp.int32, (SLOPES, SLOPES), 0) == index).astype(F32).astype(BF16)
    part = jnp.dot(difference, hot, preferred_element_type=F32)

    @pl.when(star == 0)
    def _():
        total[...] = part

    @pl.when(star > 0)
    def _():
        total[...] += part

    @pl.when(star == STARS - 1)
    def _():
        averaged = total[...] / STARS
        high = averaged.astype(BF16)
        low = (averaged - high.astype(F32)).astype(BF16)
        row = lax.broadcasted_iota(jnp.int32, (FRAMES, FRAMES), 0)
        mode = (row // 8 % 2) * 128 + (row // 16) * 8 + row % 8
        sign = (1 - 2 * parity(mode & order_ref[...])).astype(F32).astype(BF16)
        t = jnp.dot(sign, high, preferred_element_type=F32)
        t += jnp.dot(sign, low, preferred_element_type=F32)
        t_ref[0] = t[:, :HALF].astype(t_ref.dtype)
        t_ref[1] = t[:, HALF:].astype(t_ref.dtype)


def star_stage(push, pull, order, star_map):
    return pl.pallas_call(
        star_kernel,
        out_shape=jax.ShapeDtypeStruct((2, FRAMES, HALF), BF16),
        grid=(STARS,),
        in_specs=[
            pl.BlockSpec((1, FRAMES, SLOPES), lambda g: (g, 0, 0)),
            pl.BlockSpec((1, FRAMES, SLOPES), lambda g: (g, 0, 0)),
            pl.BlockSpec((1, FRAMES), lambda g: (0, 0)),
            pl.BlockSpec((STARS, SLOPES), lambda g: (0, 0)),
        ],
        out_specs=pl.BlockSpec((2, FRAMES, HALF), lambda g: (0, 0, 0)),
        scratch_shapes=[pltpu.VMEM((FRAMES, SLOPES), F32)],
        compiler_params=pltpu.CompilerParams(vmem_limit_bytes=48 * 2**20),
        name="star_stage",
    )(jnp.transpose(push, (1, 0, 2)), jnp.transpose(pull, (1, 0, 2)), order.reshape(1, -1), star_map)


def device(zh, x, y, zl, c):
    return (zh * 16 + x * 4 + y, zl * 2 + c)


def offsets(k):
    return k % 3 + (k // 9) * 3, (k // 3) % 3 + k // 9


def gram_kernel(
    t_ref,
    out_ref,
    mixed,
    row_block,
    col_block,
    pair_out,
    pair_in,
    part,
    ring_out,
    ring_in,
    final,
    final_t,
    mix_send,
    mix_recv,
    gather_send,
    gather_recv,
    pair_send,
    pair_recv,
    ring_send,
    ring_recv,
    final_send,
    final_recv,
):
    poke, sensor = lax.axis_index("poke"), lax.axis_index("sensor")
    zh, x, y = poke // 16, (poke // 4) % 4, poke % 4
    zl, c = sensor // 2, sensor % 2
    z = zh * 4 + zl

    def remote(src, dst, send, recv, target):
        return pltpu.make_async_remote_copy(
            src_ref=src, dst_ref=dst, send_sem=send, recv_sem=recv, device_id=target, device_id_type=MESH
        )

    def mix_copy(o):
        zh2, x2, y2 = (zh + 1 - o // 16) % 2, (x + (o // 4) % 4) % 4, (y + o % 4) % 4
        rows = pl.multiple_of(16 * (4 * x2 + y2), 16)
        return remote(
            t_ref.at[zh2, pl.ds(rows, 16)],
            mixed.at[pl.ds(pl.multiple_of(16 * poke, 16), 16)],
            mix_send.at[o],
            mix_recv.at[o],
            device(zh2, x2, y2, zl, c),
        )

    lax.fori_loop(0, 16, lambda o, _: (mix_copy(o).start(), 0)[1], 0)
    lax.fori_loop(17, 32, lambda o, _: (mix_copy(o).start(), 0)[1], 0)
    mixed[pl.ds(pl.multiple_of(16 * poke, 16), 16), :] = t_ref[
        zh, pl.ds(pl.multiple_of(16 * (4 * x + y), 16), 16), :
    ]
    row = lax.broadcasted_iota(jnp.int32, (ROWS, ROWS), 0)
    col = lax.broadcasted_iota(jnp.int32, (ROWS, ROWS), 1)
    sign = 1 - 2 * parity((row % 32) & (col // 16))
    sign = jnp.where(row // 32 == col % 16, sign, 0).astype(F32).astype(BF16)
    lax.fori_loop(0, 16, lambda o, _: (mix_copy(o).wait(), 0)[1], 0)
    lax.fori_loop(17, 32, lambda o, _: (mix_copy(o).wait(), 0)[1], 0)
    demodulated = jnp.dot(sign, mixed[...], preferred_element_type=F32)
    demodulated = (demodulated * (1.0 / math.sqrt(8192))).astype(BF16)
    row_block[0] = demodulated
    col_block[0] = demodulated

    gathers = []
    for d in (1, 2):
        target = device(zh, x, (y + 4 - d) % 4, zl, c)
        gathers.append(remote(row_block.at[0], row_block.at[d], gather_send.at[d], gather_recv.at[d], target))
    for d in (1, 2, 3):
        target = device(zh, (x + 4 - d) % 4, y, zl, c)
        gathers.append(
            remote(col_block.at[0], col_block.at[d], gather_send.at[2 + d], gather_recv.at[2 + d], target)
        )
    for copy in gathers:
        copy.start()
    for copy in gathers:
        copy.wait()

    def block(k):
        dx, dy = offsets(k)
        return lax.dot_general(
            row_block[dy], col_block[dx], (((1,), (1,)), ((), ())), preferred_element_type=F32
        )

    def pair_copy(kk):
        return remote(
            pair_out.at[kk], pair_in.at[kk], pair_send.at[kk], pair_recv.at[kk], device(zh, x, y, zl, 1 - c)
        )

    def give(kk, _):
        pair_out[kk] = block((1 - c) * KEPT + kk).astype(BF16)
        pair_copy(kk).start()
        return 0

    def keep(kk, _):
        value = block(c * KEPT + kk)
        pair_copy(kk).wait()
        value += pair_in[kk].astype(F32)
        for j in range(8):
            r, s = (j // 4) * 256 + (j % 2) * 128, (j // 2 % 2) * 256
            part[j, kk] = value[r : r + 128, s : s + 256]
        return 0

    lax.fori_loop(0, KEPT, give, 0)
    lax.fori_loop(0, KEPT, keep, 0)

    def ring_copy(way, d, half):
        z2 = (z + (1 if way == 0 else 7)) % 8
        return remote(
            ring_out.at[way, d, half],
            ring_in.at[way, d, half],
            ring_send.at[way, d, half],
            ring_recv.at[way, d, half],
            device(z2 // 4, x, y, z2 % 4, c),
        )

    def ring_step(way, d, half, first):
        chunk = (z + (d if way == 0 else 8 - d)) % 8
        value = part[chunk, :, half * 64 : half * 64 + 64, :]
        if not first:
            ring_copy(way, d, half).wait_recv()
            value = value + ring_in[way, d, half].astype(F32)
        ring_out[way, d - 1, half] = value.astype(BF16)
        ring_copy(way, d - 1, half).start()

    ring_step(0, 4, 0, True)
    ring_step(1, 4, 1, True)
    ring_step(0, 3, 1, True)
    ring_step(1, 3, 0, True)
    for d in (3, 2, 1):
        ring_step(0, d, 0, False)
        ring_step(1, d, 1, False)
        if d > 1:
            ring_step(0, d - 1, 1, False)
            ring_step(1, d - 1, 0, False)
    for way in (0, 1):
        for half in (0, 1):
            ring_copy(way, 0, half).wait_recv()
    for half in (0, 1):
        rows = slice(half * 64, half * 64 + 64)
        value = part[z, :, rows, :] + ring_in[0, 0, half].astype(F32) + ring_in[1, 0, half].astype(F32)
        final[:, rows, :] = value * (1.0 / math.sqrt(8192))

    zz2, b = zl // 2, zl % 2

    def ship(src, dst, send, recv, target):
        here = (target[0] == poke) & (target[1] == sensor)

        @pl.when(here)
        def _():
            pltpu.make_async_copy(src, dst, recv).start()

        @pl.when(jnp.logical_not(here))
        def _():
            remote(src, dst, send, recv, target).start()

        return here

    def shipped(src, dst, send, recv, target):
        @pl.when(jnp.logical_not((target[0] == poke) & (target[1] == sensor)))
        def _():
            remote(src, dst, send, recv, target).wait_send()

    def direct(kk):
        dx, dy = offsets(c * KEPT + kk)
        i, j = (x + dx) % 4, (y + dy) % 4
        dst = out_ref.at[pl.ds(pl.multiple_of(b * 128, 128), 128), pl.ds(pl.multiple_of(y * 256, 256), 256)]
        return (
            final.at[kk],
            dst,
            final_send.at[0, kk],
            final_recv.at[y, b],
            device(zh, x, j, 2 * zz2 + i // 2, i % 2),
        )

    def mirrored(kk):
        dx, dy = offsets(c * KEPT + kk)
        i, j = (x + dx) % 4, (y + dy) % 4
        dst = out_ref.at[:, pl.ds(pl.multiple_of(j * 256 + b * 128, 128), 128)]
        return (
            final_t.at[kk],
            dst,
            final_send.at[1, kk],
            final_recv.at[j, b],
            device(zz2, i, y, 2 * zh + x // 2, x % 2),
        )

    def has_mirror(kk):
        k = c * KEPT + kk
        return (k % 2 == 1) | (k == 4)

    for kk in range(KEPT):
        ship(*direct(kk))
    for kk in range(KEPT):

        @pl.when(has_mirror(kk))
        def _():
            final_t[kk] = final[kk].T
            ship(*mirrored(kk))

    for j in range(4):
        for half in range(2):
            pltpu.make_async_copy(final.at[0], out_ref.at[0:128, 0:256], final_recv.at[j, half]).wait()
    for kk in range(KEPT):
        shipped(*direct(kk))

        @pl.when(has_mirror(kk))
        def _():
            shipped(*mirrored(kk))

    for d in (3, 2, 1, 0):
        for way in (0, 1):
            for half in (0, 1):
                if d < 3 or way == half:
                    ring_copy(way, d, half).wait_send()


def gram_stage(t):
    dma = pltpu.SemaphoreType.DMA
    return pl.pallas_call(
        gram_kernel,
        out_shape=jax.ShapeDtypeStruct((256, 1024), F32),
        in_specs=[pl.BlockSpec(memory_space=pltpu.VMEM)],
        out_specs=pl.BlockSpec(memory_space=pltpu.VMEM),
        scratch_shapes=[
            pltpu.VMEM((ROWS, HALF), BF16),
            pltpu.VMEM((3, ROWS, HALF), BF16),
            pltpu.VMEM((4, ROWS, HALF), BF16),
            pltpu.VMEM((KEPT, ROWS, ROWS), BF16),
            pltpu.VMEM((KEPT, ROWS, ROWS), BF16),
            pltpu.VMEM((8, KEPT, 128, 256), F32),
            pltpu.VMEM((2, 4, 2, KEPT, 64, 256), BF16),
            pltpu.VMEM((2, 4, 2, KEPT, 64, 256), BF16),
            pltpu.VMEM((KEPT, 128, 256), F32),
            pltpu.VMEM((KEPT, 256, 128), F32),
            dma((32,)),
            dma((32,)),
            dma((6,)),
            dma((6,)),
            dma((KEPT,)),
            dma((KEPT,)),
            dma((2, 4, 2)),
            dma((2, 4, 2)),
            dma((2, KEPT)),
            dma((4, 2)),
        ],
        compiler_params=pltpu.CompilerParams(has_side_effects=True, vmem_limit_bytes=48 * 2**20),
        name="gram_stage",
    )(t)


def local(push_slopes, pull_slopes, pattern_order, star_map):
    return gram_stage(star_stage(push_slopes, pull_slopes, pattern_order, star_map))


def solution(mesh):
    return jax.shard_map(
        local,
        mesh=mesh,
        in_specs=(P("poke", None, "sensor"), P("poke", None, "sensor"), P(), P(None, "sensor")),
        out_specs=P("poke", "sensor"),
        check_vma=False,
    )
```

```python
import functools
import math

import jax
import jax.numpy as jnp
from jax import lax
from jax.experimental import pallas as pl
from jax.experimental.pallas import tpu as pltpu
from jax.sharding import PartitionSpec as P

MESH = pl.DeviceIdType.MESH
STARS, FRAMES, SLOPES = 6, 256, 1024
HALF = SLOPES // 2
ROWS = 512
KEPT = 5
F32, BF16 = jnp.float32, jnp.bfloat16
SENT = BF16
PIECES = 2
WIDTH = HALF // PIECES


def parity(bits):
    for shift in (4, 2, 1):
        bits = bits ^ (bits >> shift)
    return bits & 1


def device(zh, x, y, zl, c):
    return (zh * 16 + x * 4 + y, zl * 2 + c)


BLOCKS = (((0, 0), (0, 1), (3, 1), (0, 2), (1, 2)), ((1, 0), (1, 1), (2, 0), (2, 1), (2, 2)))


GROUPS = ((0, 1), (1, 2), (2, 3), (3, 4), (4, 5))


def is_computed(dx, dy):
    return jnp.where(((dx < 3) & (dy < 3)) | ((dx == 3) & (dy == 1)), 1, 0)


def is_mirrored(dx, dy):
    return (dx % 2, dy % 2) != (0, 0)


def demodulation_kernel(
    push_ref,
    pull_ref,
    order_hbm,
    map_hbm,
    out_ref,
    push,
    pull,
    order_ref,
    map_ref,
    difference,
    total,
    transformed,
    mixed,
    row_block,
    col_block,
    pair_out,
    pair_in,
    part,
    ring_out,
    ring_in,
    final_out,
    final_in,
    load_sem,
    table_sem,
    mix_send,
    mix_recv,
    gather_send,
    gather_recv,
    pair_send,
    pair_recv,
    ring_send,
    ring_recv,
    final_send,
    final_recv,
):
    poke, sensor = lax.axis_index("poke"), lax.axis_index("sensor")
    zh, x, y = poke // 16, (poke // 4) % 4, poke % 4
    zl, c = sensor // 2, sensor % 2
    z = zh * 4 + zl
    zz2, b = zl // 2, zl % 2

    def remote(src, dst, send, recv, target):
        return pltpu.make_async_remote_copy(
            src_ref=src, dst_ref=dst, send_sem=send, recv_sem=recv, device_id=target, device_id_type=MESH
        )

    def load(star):
        return (
            pltpu.make_async_copy(push_ref.at[star], push.at[star], load_sem.at[0, star]),
            pltpu.make_async_copy(pull_ref.at[star], pull.at[star], load_sem.at[1, star]),
        )

    tables = [
        pltpu.make_async_copy(order_hbm, order_ref, table_sem.at[0]),
        pltpu.make_async_copy(map_hbm, map_ref, table_sem.at[1]),
    ]
    for copy in tables:
        copy.start()

    def start_load(star, _):
        for copy in load(star):
            copy.start()
        return 0

    lax.fori_loop(0, STARS, start_load, 0)

    barrier = pltpu.get_barrier_semaphore()

    def greet(target):
        pl.semaphore_signal(barrier, inc=1, device_id=target, device_id_type=MESH)

    def mix_target(o):
        return (zh + 1 - o // 16) % 2, (x + (o // 4) % 4) % 4, (y + o % 4) % 4

    def greet_mix(o, _):
        zh2, x2, y2 = mix_target(o)
        greet(device(zh2, x2, y2, zl, c))
        return 0

    def greet_direct(o, _):
        greet(device(zh, x, (y + o // 4) % 4, 2 * zz2 + (b + o // 2) % 2, (c + o) % 2))
        return 0

    def greet_mirror(o, _):
        greet(device(zz2, (x + o // 4) % 4, y, 2 * zh + (b + o // 2) % 2, (c + o) % 2))
        return 0

    lax.fori_loop(0, 16, greet_mix, 0)
    lax.fori_loop(17, 32, greet_mix, 0)
    lax.fori_loop(1, 16, greet_direct, 0)
    lax.fori_loop(1, 16, greet_mirror, 0)
    for step in (1, 7):
        greet(device((z + step) % 8 // 4, x, y, (z + step) % 4, c))

    @pl.when(zz2 != zh)
    def _():
        greet(device(zz2, x, y, 2 * zh + b, c))

    for copy in tables:
        copy.wait()
    row = lax.broadcasted_iota(jnp.int32, (FRAMES, FRAMES), 0)
    mode = (row // 8 % 2) * 128 + (row // 16) * 8 + row % 8
    local_sign = (1 - 2 * parity(mode & order_ref[...])).astype(F32).astype(BF16)

    def average(half, piece, first):
        def star_step(star, _):
            if first:
                for copy in load(star):
                    copy.wait()
                difference[star] = (push[star].astype(F32) - pull[star].astype(F32)).astype(BF16)
            columns = pl.ds(pl.multiple_of(half * HALF + piece * WIDTH, 128), WIDTH)
            index = map_ref[pl.ds(star, 1), columns] % SLOPES
            hot = (lax.broadcasted_iota(jnp.int32, (SLOPES, WIDTH), 0) == index).astype(F32).astype(BF16)
            total[...] += jnp.dot(difference[star], hot, preferred_element_type=F32)
            return 0

        total[...] = jnp.zeros_like(total)
        lax.fori_loop(0, STARS, star_step, 0)
        averaged = total[...] / STARS
        high = averaged.astype(BF16)
        low = (averaged - high.astype(F32)).astype(BF16)
        t = jnp.dot(local_sign, high, preferred_element_type=F32)
        t += jnp.dot(local_sign, low, preferred_element_type=F32)
        transformed[half, piece] = t.astype(BF16)

    def mix_copy(piece, o):
        zh2, x2, y2 = mix_target(o)
        rows = pl.multiple_of(16 * (4 * x2 + y2), 16)
        return remote(
            transformed.at[zh2, piece, pl.ds(rows, 16)],
            mixed.at[piece, pl.ds(pl.multiple_of(16 * poke, 16), 16)],
            mix_send.at[piece, o],
            mix_recv.at[piece, o],
            device(zh2, x2, y2, zl, c),
        )

    def start_mix(piece, lo, hi):
        lax.fori_loop(lo, hi, lambda o, _: (mix_copy(piece, o).start(), 0)[1], 0)

    def wait_mix(piece, lo, hi):
        lax.fori_loop(lo, hi, lambda o, _: (mix_copy(piece, o).wait(), 0)[1], 0)

    for piece in range(PIECES):
        average(1 - zh, piece, piece == 0)
        if piece == 0:
            pl.semaphore_wait(barrier, 31 + 15 + 15 + 2 + jnp.where(zz2 != zh, 1, 0))
        start_mix(piece, 0, 16)
        average(zh, piece, False)
        start_mix(piece, 17, 32)
        mixed[piece, pl.ds(pl.multiple_of(16 * poke, 16), 16), :] = transformed[
            zh, piece, pl.ds(pl.multiple_of(16 * (4 * x + y), 16), 16), :
        ]

    row = lax.broadcasted_iota(jnp.int32, (ROWS, ROWS), 0)
    col = lax.broadcasted_iota(jnp.int32, (ROWS, ROWS), 1)
    sign = 1 - 2 * parity((row % 32) & (col // 16))
    sign = jnp.where(row // 32 == col % 16, sign, 0).astype(F32).astype(BF16)

    def row_copy(piece, d):
        target = device(zh, x, (y + 4 - d) % 4, zl, c)
        return remote(
            row_block.at[0, piece],
            row_block.at[d, piece],
            gather_send.at[piece, d],
            gather_recv.at[piece, d],
            target,
        )

    def col_copy(piece, d):
        target = device(zh, (x + 4 - d) % 4, y, zl, c)
        return remote(
            col_block.at[0, piece],
            col_block.at[d, piece],
            gather_send.at[piece, 2 + d],
            gather_recv.at[piece, 2 + d],
            target,
        )

    near, far_col, far_row = [], [], []
    for piece in range(PIECES):
        wait_mix(piece, 0, 16)
        wait_mix(piece, 17, 32)
        demodulated = jnp.dot(sign, mixed[piece], preferred_element_type=F32)
        demodulated = (demodulated * (1.0 / math.sqrt(8192))).astype(BF16)
        row_block[0, piece] = demodulated
        col_block[0, piece] = demodulated
        for copy in (col_copy(piece, 1), row_copy(piece, 1), col_copy(piece, 3)):
            copy.start()
            near.append(copy)
    for piece in range(PIECES):
        far_col.append(col_copy(piece, 2))
        far_row.append(row_copy(piece, 2))
        far_col[-1].start()
        far_row[-1].start()

    def pick(core, tau):
        (dx0, dy0), (dx1, dy1) = BLOCKS[0][tau], BLOCKS[1][tau]
        return dx0 + core * (dx1 - dx0), dy0 + core * (dy1 - dy0)

    def block(core, tau):
        dx, dy = pick(core, tau)
        value = None
        for piece in range(PIECES):
            term = lax.dot_general(
                row_block[dy, piece],
                col_block[dx, piece],
                (((1,), (1,)), ((), ())),
                preferred_element_type=F32,
            )
            value = term if value is None else value + term
        return value

    def pair_copy(tau):
        return remote(
            pair_out.at[tau], pair_in.at[tau], pair_send.at[tau], pair_recv.at[tau], device(zh, x, y, zl, 1 - c)
        )

    def ring_copy(g, way, d, half):
        z2 = (z + (1 if way == 0 else 7)) % 8
        lo, hi = GROUPS[g]
        return remote(
            ring_out.at[way, d, half, lo:hi],
            ring_in.at[way, d, half, lo:hi],
            ring_send.at[g, way, d, half],
            ring_recv.at[g, way, d, half],
            device(z2 // 4, x, y, z2 % 4, c),
        )

    def ring_step(g, way, d, half, first=False):
        lo, hi = GROUPS[g]
        chunk = (z + (d if way == 0 else 8 - d)) % 8
        value = part[lo:hi, chunk, half * 64 : half * 64 + 64, :]
        if not first:
            ring_copy(g, way, d, half).wait_recv()
            value = value + ring_in[way, d, half, lo:hi].astype(F32)
        ring_out[way, d - 1, half, lo:hi] = value.astype(BF16)
        ring_copy(g, way, d - 1, half).start()

    def give(tau):
        pair_out[tau] = block(1 - c, tau).astype(BF16)
        pair_copy(tau).start()

    def keep(tau):
        value = block(c, tau)
        pair_copy(tau).wait_recv()
        value += pair_in[tau].astype(F32)
        for j in range(8):
            r, s = (j // 4) * 256 + (j % 2) * 128, (j // 2 % 2) * 256
            part[tau, j] = value[r : r + 128, s : s + 256]

    def begin(g):
        ring_step(g, 0, 4, 0, True)
        ring_step(g, 1, 4, 1, True)
        ring_step(g, 0, 3, 1, True)
        ring_step(g, 1, 3, 0, True)

    def progress(g, d):
        ring_step(g, 0, d, 0)
        ring_step(g, 1, d, 1)
        if d > 1:
            ring_step(g, 0, d - 1, 1)
            ring_step(g, 1, d - 1, 0)

    def is_here(target):
        return (target[0] == poke) & (target[1] == sensor)

    def ship(src, dst, send, recv, target):
        here = is_here(target)

        @pl.when(here)
        def _():
            pltpu.make_async_copy(src, dst, recv).start()

        @pl.when(jnp.logical_not(here))
        def _():
            remote(src, dst, send, recv, target).start()

    def shipped(src, dst, send, recv, target):
        @pl.when(jnp.logical_not(is_here(target)))
        def _():
            remote(src, dst, send, recv, target).wait_send()

    def direct(tau):
        dx, dy = pick(c, tau)
        i, j = (x + dx) % 4, (y + dy) % 4
        target = device(zh, x, j, 2 * zz2 + i // 2, i % 2)
        return final_out.at[0, tau], final_in.at[y, b], final_send.at[0, tau], final_recv.at[y, b], target

    def mirrored(tau):
        dx, dy = pick(c, tau)
        i, j = (x + dx) % 4, (y + dy) % 4
        target = device(zz2, i, y, 2 * zh + x // 2, x % 2)
        return final_out.at[1, tau], final_in.at[j, b], final_send.at[1, tau], final_recv.at[j, b], target

    def when_mirrored(tau, action):
        cores = [core for core in (0, 1) if is_mirrored(*BLOCKS[core][tau])]
        if len(cores) == 2:
            action()
        elif cores:
            pl.when(c == cores[0])(action)

    def finish(g):
        for way in (0, 1):
            for half in (0, 1):
                ring_copy(g, way, 0, half).wait_recv()
        for tau in range(*GROUPS[g]):
            value = part[tau, z] + ring_in[0, 0, :, tau].reshape(128, 256).astype(F32)
            value += ring_in[1, 0, :, tau].reshape(128, 256).astype(F32)
            value *= 1.0 / math.sqrt(8192)
            final_out[0, tau, 0] = value[:, :128].astype(SENT)
            final_out[0, tau, 1] = value[:, 128:].astype(SENT)
            ship(*direct(tau))

            def send_mirror(tau=tau, value=value):
                final_out[1, tau, 0] = value[:, :128].T.astype(SENT)
                final_out[1, tau, 1] = value[:, 128:].T.astype(SENT)
                ship(*mirrored(tau))

            when_mirrored(tau, send_mirror)

    for copy in near:
        copy.wait_recv()
    give(0)
    give(1)
    keep(0)
    begin(0)
    keep(1)
    begin(1)
    for d in (3, 2):
        progress(0, d)
        progress(1, d)
    for copy in far_col:
        copy.wait_recv()
    give(2)
    progress(0, 1)
    progress(1, 1)
    keep(2)
    begin(2)
    for copy in far_row:
        copy.wait_recv()
    give(3)
    give(4)
    finish(0)
    keep(3)
    begin(3)
    finish(1)
    keep(4)
    begin(4)
    for d in (3, 2, 1):
        for g in (2, 3, 4):
            progress(g, d)
    for g in (2, 3, 4):
        finish(g)

    for j in range(4):
        direct_in = is_computed((sensor - 4 * zz2 - x + 4) % 4, (y - j + 4) % 4)
        for half in range(2):
            pltpu.make_async_copy(final_out.at[0, 0], final_in.at[j, half], final_recv.at[j, half]).wait()
            for w in range(2):
                rows = half * direct_in + w * (1 - direct_in)
                cols = w * direct_in + half * (1 - direct_in)
                out_ref[
                    pl.ds(pl.multiple_of(rows * 128, 128), 128),
                    pl.ds(pl.multiple_of(j * 256 + cols * 128, 128), 128),
                ] = final_in[j, half, w].astype(F32)

    for copy in near + far_col + far_row:
        copy.wait_send()
    for g in range(len(GROUPS)):
        for d in (3, 2, 1, 0):
            for way in (0, 1):
                for half in (0, 1):
                    if d < 3 or way == half:
                        ring_copy(g, way, d, half).wait_send()
    for tau in range(KEPT):
        pair_copy(tau).wait_send()
        shipped(*direct(tau))
        when_mirrored(tau, lambda tau=tau: shipped(*mirrored(tau)))


def local(push_slopes, pull_slopes, pattern_order, star_map):
    dma = pltpu.SemaphoreType.DMA
    vmem = pl.BlockSpec(memory_space=pltpu.VMEM)
    hbm = pl.BlockSpec(memory_space=pl.ANY)
    return pl.pallas_call(
        demodulation_kernel,
        out_shape=jax.ShapeDtypeStruct((256, 1024), F32),
        in_specs=[hbm] * 4,
        out_specs=vmem,
        scratch_shapes=[
            pltpu.VMEM((STARS, FRAMES, SLOPES), BF16),
            pltpu.VMEM((STARS, FRAMES, SLOPES), BF16),
            pltpu.VMEM((1, FRAMES), jnp.int32),
            pltpu.VMEM((STARS, SLOPES), jnp.int32),
            pltpu.VMEM((STARS, FRAMES, SLOPES), BF16),
            pltpu.VMEM((FRAMES, WIDTH), F32),
            pltpu.VMEM((2, PIECES, FRAMES, WIDTH), BF16),
            pltpu.VMEM((PIECES, ROWS, WIDTH), BF16),
            pltpu.VMEM((3, PIECES, ROWS, WIDTH), BF16),
            pltpu.VMEM((4, PIECES, ROWS, WIDTH), BF16),
            pltpu.VMEM((KEPT, ROWS, ROWS), BF16),
            pltpu.VMEM((KEPT, ROWS, ROWS), BF16),
            pltpu.VMEM((KEPT, 8, 128, 256), F32),
            pltpu.VMEM((2, 4, 2, KEPT, 64, 256), BF16),
            pltpu.VMEM((2, 4, 2, KEPT, 64, 256), BF16),
            pltpu.VMEM((2, KEPT, 2, 128, 128), SENT),
            pltpu.VMEM((4, 2, 2, 128, 128), SENT),
            dma((2, STARS)),
            dma((2,)),
            dma((PIECES, 32)),
            dma((PIECES, 32)),
            dma((PIECES, 6)),
            dma((PIECES, 6)),
            dma((KEPT,)),
            dma((KEPT,)),
            dma((len(GROUPS), 2, 4, 2)),
            dma((len(GROUPS), 2, 4, 2)),
            dma((2, KEPT)),
            dma((4, 2)),
        ],
        compiler_params=pltpu.CompilerParams(
            collective_id=0, has_side_effects=True, vmem_limit_bytes=56 * 2**20
        ),
        name="demodulation",
    )(
        jnp.transpose(push_slopes, (1, 0, 2)),
        jnp.transpose(pull_slopes, (1, 0, 2)),
        pattern_order.reshape(1, -1),
        star_map,
    )


def solution(mesh):
    return jax.shard_map(
        local,
        mesh=mesh,
        in_specs=(P("poke", None, "sensor"), P("poke", None, "sensor"), P(), P(None, "sensor")),
        out_specs=P("poke", "sensor"),
        check_vma=False,
    )
```

```python
import functools
import math

import jax
import jax.numpy as jnp
from jax import lax
from jax.experimental import pallas as pl
from jax.experimental.pallas import tpu as pltpu
from jax.sharding import PartitionSpec as P

MESH = pl.DeviceIdType.MESH
STARS, FRAMES, SLOPES = 6, 256, 1024
HALF = SLOPES // 2
ROWS = 512
KEPT = 5
F32, BF16 = jnp.float32, jnp.bfloat16
SENT = BF16
PIECES = 2
WIDTH = HALF // PIECES


def parity(bits):
    for shift in (4, 2, 1):
        bits = bits ^ (bits >> shift)
    return bits & 1


def device(zh, x, y, zl, c):
    return (zh * 16 + x * 4 + y, zl * 2 + c)


BLOCKS = (((0, 0), (0, 1), (3, 1), (0, 2), (1, 2)), ((1, 0), (1, 1), (2, 0), (2, 1), (2, 2)))


GROUPS = ((0, 1), (1, 2), (2, 3), (3, 4), (4, 5))


def is_computed(dx, dy):
    return jnp.where(((dx < 3) & (dy < 3)) | ((dx == 3) & (dy == 1)), 1, 0)


def is_mirrored(dx, dy):
    return (dx % 2, dy % 2) != (0, 0)


def demodulation_kernel(
    push_ref,
    pull_ref,
    order_hbm,
    map_hbm,
    out_ref,
    push,
    pull,
    order_ref,
    map_ref,
    difference,
    total,
    transformed,
    mixed,
    row_block,
    col_block,
    pair_out,
    pair_in,
    part,
    ring_out,
    ring_in,
    final_out,
    final_in,
    load_sem,
    table_sem,
    mix_send,
    mix_recv,
    gather_send,
    gather_recv,
    pair_send,
    pair_recv,
    ring_send,
    ring_recv,
    final_send,
    final_recv,
):
    poke, sensor = lax.axis_index("poke"), lax.axis_index("sensor")
    zh, x, y = poke // 16, (poke // 4) % 4, poke % 4
    zl, c = sensor // 2, sensor % 2
    z = zh * 4 + zl
    zz2, b = zl // 2, zl % 2

    def remote(src, dst, send, recv, target):
        return pltpu.make_async_remote_copy(
            src_ref=src, dst_ref=dst, send_sem=send, recv_sem=recv, device_id=target, device_id_type=MESH
        )

    def load(star):
        return (
            pltpu.make_async_copy(push_ref.at[star], push.at[star], load_sem.at[0, star]),
            pltpu.make_async_copy(pull_ref.at[star], pull.at[star], load_sem.at[1, star]),
        )

    tables = [
        pltpu.make_async_copy(order_hbm, order_ref, table_sem.at[0]),
        pltpu.make_async_copy(map_hbm, map_ref, table_sem.at[1]),
    ]
    for copy in tables:
        copy.start()

    def start_load(star, _):
        for copy in load(star):
            copy.start()
        return 0

    lax.fori_loop(0, STARS, start_load, 0)

    barrier = pltpu.get_barrier_semaphore()

    def greet(target):
        pl.semaphore_signal(barrier, inc=1, device_id=target, device_id_type=MESH)

    def mix_target(o):
        return (zh + 1 - o // 16) % 2, (x + (o // 4) % 4) % 4, (y + o % 4) % 4

    def greet_mix(o, _):
        zh2, x2, y2 = mix_target(o)
        greet(device(zh2, x2, y2, zl, c))
        return 0

    def greet_direct(o, _):
        greet(device(zh, x, (y + o // 4) % 4, 2 * zz2 + (b + o // 2) % 2, (c + o) % 2))
        return 0

    def greet_mirror(o, _):
        greet(device(zz2, (x + o // 4) % 4, y, 2 * zh + (b + o // 2) % 2, (c + o) % 2))
        return 0

    lax.fori_loop(0, 16, greet_mix, 0)
    lax.fori_loop(17, 32, greet_mix, 0)
    lax.fori_loop(1, 16, greet_direct, 0)
    lax.fori_loop(1, 16, greet_mirror, 0)
    for step in (1, 7):
        greet(device((z + step) % 8 // 4, x, y, (z + step) % 4, c))

    @pl.when(zz2 != zh)
    def _():
        greet(device(zz2, x, y, 2 * zh + b, c))

    for copy in tables:
        copy.wait()
    row = lax.broadcasted_iota(jnp.int32, (FRAMES, FRAMES), 0)
    mode = (row // 8 % 2) * 128 + (row // 16) * 8 + row % 8
    local_sign = (1 - 2 * parity(mode & order_ref[...])).astype(F32).astype(BF16)

    def average(half, piece, first):
        def star_step(star, _):
            if first:
                for copy in load(star):
                    copy.wait()
                difference[star] = (push[star].astype(F32) - pull[star].astype(F32)).astype(BF16)
            columns = pl.ds(pl.multiple_of(half * HALF + piece * WIDTH, 128), WIDTH)
            index = jnp.where(lax.broadcasted_iota(jnp.int32, (STARS, WIDTH), 0) == star, map_ref[:, columns], 0)
            index = jnp.sum(index, axis=0, keepdims=True) % SLOPES
            hot = (lax.broadcasted_iota(jnp.int32, (SLOPES, WIDTH), 0) == index).astype(F32).astype(BF16)
            total[...] += jnp.dot(difference[star], hot, preferred_element_type=F32)
            return 0

        total[...] = jnp.zeros_like(total)
        lax.fori_loop(0, STARS, star_step, 0)
        averaged = total[...] / STARS
        high = averaged.astype(BF16)
        low = (averaged - high.astype(F32)).astype(BF16)
        t = jnp.dot(local_sign, high, preferred_element_type=F32)
        t += jnp.dot(local_sign, low, preferred_element_type=F32)
        transformed[half, piece] = t.astype(BF16)

    def mix_copy(piece, o):
        zh2, x2, y2 = mix_target(o)
        rows = pl.multiple_of(16 * (4 * x2 + y2), 16)
        return remote(
            transformed.at[zh2, piece, pl.ds(rows, 16)],
            mixed.at[piece, pl.ds(pl.multiple_of(16 * poke, 16), 16)],
            mix_send.at[piece, o],
            mix_recv.at[piece, o],
            device(zh2, x2, y2, zl, c),
        )

    def start_mix(piece, lo, hi):
        lax.fori_loop(lo, hi, lambda o, _: (mix_copy(piece, o).start(), 0)[1], 0)

    def wait_mix(piece, lo, hi):
        lax.fori_loop(lo, hi, lambda o, _: (mix_copy(piece, o).wait(), 0)[1], 0)

    for piece in range(PIECES):
        average(1 - zh, piece, piece == 0)
        if piece == 0:
            pl.semaphore_wait(barrier, 31 + 15 + 15 + 2 + jnp.where(zz2 != zh, 1, 0))
        start_mix(piece, 0, 16)
        average(zh, piece, False)
        start_mix(piece, 17, 32)
        mixed[piece, pl.ds(pl.multiple_of(16 * poke, 16), 16), :] = transformed[
            zh, piece, pl.ds(pl.multiple_of(16 * (4 * x + y), 16), 16), :
        ]

    row = lax.broadcasted_iota(jnp.int32, (ROWS, ROWS), 0)
    col = lax.broadcasted_iota(jnp.int32, (ROWS, ROWS), 1)
    sign = 1 - 2 * parity((row % 32) & (col // 16))
    sign = jnp.where(row // 32 == col % 16, sign, 0).astype(F32).astype(BF16)

    def row_copy(piece, d):
        target = device(zh, x, (y + 4 - d) % 4, zl, c)
        return remote(
            row_block.at[0, piece],
            row_block.at[d, piece],
            gather_send.at[piece, d],
            gather_recv.at[piece, d],
            target,
        )

    def col_copy(piece, d):
        target = device(zh, (x + 4 - d) % 4, y, zl, c)
        return remote(
            col_block.at[0, piece],
            col_block.at[d, piece],
            gather_send.at[piece, 2 + d],
            gather_recv.at[piece, 2 + d],
            target,
        )

    near, far_col, far_row = [], [], []
    for piece in range(PIECES):
        wait_mix(piece, 0, 16)
        wait_mix(piece, 17, 32)
        demodulated = jnp.dot(sign, mixed[piece], preferred_element_type=F32)
        demodulated = (demodulated * (1.0 / math.sqrt(8192))).astype(BF16)
        row_block[0, piece] = demodulated
        col_block[0, piece] = demodulated
        for copy in (col_copy(piece, 1), row_copy(piece, 1), col_copy(piece, 3)):
            copy.start()
            near.append(copy)
    for piece in range(PIECES):
        far_col.append(col_copy(piece, 2))
        far_row.append(row_copy(piece, 2))

    def pick(core, tau):
        (dx0, dy0), (dx1, dy1) = BLOCKS[0][tau], BLOCKS[1][tau]
        return dx0 + core * (dx1 - dx0), dy0 + core * (dy1 - dy0)

    def block(core, tau):
        dx, dy = pick(core, tau)
        value = None
        for piece in range(PIECES):
            term = lax.dot_general(
                row_block[dy, piece],
                col_block[dx, piece],
                (((1,), (1,)), ((), ())),
                preferred_element_type=F32,
            )
            value = term if value is None else value + term
        return value

    def pair_copy(tau):
        return remote(
            pair_out.at[tau], pair_in.at[tau], pair_send.at[tau], pair_recv.at[tau], device(zh, x, y, zl, 1 - c)
        )

    def ring_copy(g, way, d, half):
        z2 = (z + (1 if way == 0 else 7)) % 8
        lo, hi = GROUPS[g]
        return remote(
            ring_out.at[way, d, half, lo:hi],
            ring_in.at[way, d, half, lo:hi],
            ring_send.at[g, way, d, half],
            ring_recv.at[g, way, d, half],
            device(z2 // 4, x, y, z2 % 4, c),
        )

    def ring_step(g, way, d, half, first=False):
        lo, hi = GROUPS[g]
        chunk = (z + (d if way == 0 else 8 - d)) % 8
        value = part[lo:hi, chunk, half * 64 : half * 64 + 64, :]
        if not first:
            ring_copy(g, way, d, half).wait_recv()
            value = value + ring_in[way, d, half, lo:hi].astype(F32)
        ring_out[way, d - 1, half, lo:hi] = value.astype(BF16)
        ring_copy(g, way, d - 1, half).start()

    def give(tau):
        pair_out[tau] = block(1 - c, tau).astype(BF16)
        pair_copy(tau).start()

    def keep(tau):
        value = block(c, tau)
        pair_copy(tau).wait_recv()
        value += pair_in[tau].astype(F32)
        for j in range(8):
            r, s = (j // 4) * 256 + (j % 2) * 128, (j // 2 % 2) * 256
            part[tau, j] = value[r : r + 128, s : s + 256]

    def begin(g):
        ring_step(g, 0, 4, 0, True)
        ring_step(g, 1, 4, 1, True)
        ring_step(g, 0, 3, 1, True)
        ring_step(g, 1, 3, 0, True)

    def progress(g, d):
        ring_step(g, 0, d, 0)
        ring_step(g, 1, d, 1)
        if d > 1:
            ring_step(g, 0, d - 1, 1)
            ring_step(g, 1, d - 1, 0)

    def is_here(target):
        return (target[0] == poke) & (target[1] == sensor)

    def ship(src, dst, send, recv, target):
        here = is_here(target)

        @pl.when(here)
        def _():
            pltpu.make_async_copy(src, dst, recv).start()

        @pl.when(jnp.logical_not(here))
        def _():
            remote(src, dst, send, recv, target).start()

    def shipped(src, dst, send, recv, target):
        @pl.when(jnp.logical_not(is_here(target)))
        def _():
            remote(src, dst, send, recv, target).wait_send()

    def direct(tau):
        dx, dy = pick(c, tau)
        i, j = (x + dx) % 4, (y + dy) % 4
        target = device(zh, x, j, 2 * zz2 + i // 2, i % 2)
        return final_out.at[0, tau], final_in.at[y, b], final_send.at[0, tau], final_recv.at[y, b], target

    def mirrored(tau):
        dx, dy = pick(c, tau)
        i, j = (x + dx) % 4, (y + dy) % 4
        target = device(zz2, i, y, 2 * zh + x // 2, x % 2)
        return final_out.at[1, tau], final_in.at[j, b], final_send.at[1, tau], final_recv.at[j, b], target

    def when_mirrored(tau, action):
        cores = [core for core in (0, 1) if is_mirrored(*BLOCKS[core][tau])]
        if len(cores) == 2:
            action()
        elif cores:
            pl.when(c == cores[0])(action)

    def finish(g):
        for way in (0, 1):
            for half in (0, 1):
                ring_copy(g, way, 0, half).wait_recv()
        for tau in range(*GROUPS[g]):
            value = part[tau, z] + ring_in[0, 0, :, tau].reshape(128, 256).astype(F32)
            value += ring_in[1, 0, :, tau].reshape(128, 256).astype(F32)
            value *= 1.0 / math.sqrt(8192)
            final_out[0, tau, 0] = value[:, :128].astype(SENT)
            final_out[0, tau, 1] = value[:, 128:].astype(SENT)
            ship(*direct(tau))

            def send_mirror(tau=tau, value=value):
                final_out[1, tau, 0] = value[:, :128].T.astype(SENT)
                final_out[1, tau, 1] = value[:, 128:].T.astype(SENT)
                ship(*mirrored(tau))

            when_mirrored(tau, send_mirror)

    for copy in near:
        copy.wait_recv()
    for copy in far_col + far_row:
        copy.start()
    give(0)
    give(1)
    keep(0)
    begin(0)
    keep(1)
    begin(1)
    for d in (3, 2):
        progress(0, d)
        progress(1, d)
    for copy in far_col:
        copy.wait_recv()
    give(2)
    progress(0, 1)
    progress(1, 1)
    keep(2)
    begin(2)
    for copy in far_row:
        copy.wait_recv()
    give(3)
    give(4)
    finish(0)
    keep(3)
    begin(3)
    finish(1)
    keep(4)
    begin(4)
    for d in (3, 2, 1):
        for g in (2, 3, 4):
            progress(g, d)
    for g in (2, 3, 4):
        finish(g)

    for j in range(4):
        direct_in = is_computed((sensor - 4 * zz2 - x + 4) % 4, (y - j + 4) % 4)
        for half in range(2):
            pltpu.make_async_copy(final_out.at[0, 0], final_in.at[j, half], final_recv.at[j, half]).wait()
            for w in range(2):
                rows = half * direct_in + w * (1 - direct_in)
                cols = w * direct_in + half * (1 - direct_in)
                out_ref[
                    pl.ds(pl.multiple_of(rows * 128, 128), 128),
                    pl.ds(pl.multiple_of(j * 256 + cols * 128, 128), 128),
                ] = final_in[j, half, w].astype(F32)

    for copy in near + far_col + far_row:
        copy.wait_send()
    for g in range(len(GROUPS)):
        for d in (3, 2, 1, 0):
            for way in (0, 1):
                for half in (0, 1):
                    if d < 3 or way == half:
                        ring_copy(g, way, d, half).wait_send()
    for tau in range(KEPT):
        pair_copy(tau).wait_send()
        shipped(*direct(tau))
        when_mirrored(tau, lambda tau=tau: shipped(*mirrored(tau)))


def local(push_slopes, pull_slopes, pattern_order, star_map):
    dma = pltpu.SemaphoreType.DMA
    vmem = pl.BlockSpec(memory_space=pltpu.VMEM)
    hbm = pl.BlockSpec(memory_space=pl.ANY)
    return pl.pallas_call(
        demodulation_kernel,
        out_shape=jax.ShapeDtypeStruct((256, 1024), F32),
        in_specs=[hbm] * 4,
        out_specs=vmem,
        scratch_shapes=[
            pltpu.VMEM((STARS, FRAMES, SLOPES), BF16),
            pltpu.VMEM((STARS, FRAMES, SLOPES), BF16),
            pltpu.VMEM((1, FRAMES), jnp.int32),
            pltpu.VMEM((STARS, SLOPES), jnp.int32),
            pltpu.VMEM((STARS, FRAMES, SLOPES), BF16),
            pltpu.VMEM((FRAMES, WIDTH), F32),
            pltpu.VMEM((2, PIECES, FRAMES, WIDTH), BF16),
            pltpu.VMEM((PIECES, ROWS, WIDTH), BF16),
            pltpu.VMEM((3, PIECES, ROWS, WIDTH), BF16),
            pltpu.VMEM((4, PIECES, ROWS, WIDTH), BF16),
            pltpu.VMEM((KEPT, ROWS, ROWS), BF16),
            pltpu.VMEM((KEPT, ROWS, ROWS), BF16),
            pltpu.VMEM((KEPT, 8, 128, 256), F32),
            pltpu.VMEM((2, 4, 2, KEPT, 64, 256), BF16),
            pltpu.VMEM((2, 4, 2, KEPT, 64, 256), BF16),
            pltpu.VMEM((2, KEPT, 2, 128, 128), SENT),
            pltpu.VMEM((4, 2, 2, 128, 128), SENT),
            dma((2, STARS)),
            dma((2,)),
            dma((PIECES, 32)),
            dma((PIECES, 32)),
            dma((PIECES, 6)),
            dma((PIECES, 6)),
            dma((KEPT,)),
            dma((KEPT,)),
            dma((len(GROUPS), 2, 4, 2)),
            dma((len(GROUPS), 2, 4, 2)),
            dma((2, KEPT)),
            dma((4, 2)),
        ],
        compiler_params=pltpu.CompilerParams(
            collective_id=0, has_side_effects=True, vmem_limit_bytes=56 * 2**20
        ),
        name="demodulation",
    )(
        jnp.transpose(push_slopes, (1, 0, 2)),
        jnp.transpose(pull_slopes, (1, 0, 2)),
        pattern_order.reshape(1, -1),
        star_map,
    )


def solution(mesh):
    return jax.shard_map(
        local,
        mesh=mesh,
        in_specs=(P("poke", None, "sensor"), P("poke", None, "sensor"), P(), P(None, "sensor")),
        out_specs=P("poke", "sensor"),
        check_vma=False,
    )
```

```python
import functools
import math

import jax
import jax.numpy as jnp
from jax import lax
from jax.experimental import pallas as pl
from jax.experimental.pallas import tpu as pltpu
from jax.sharding import PartitionSpec as P

MESH = pl.DeviceIdType.MESH
STARS, FRAMES, SLOPES = 6, 256, 1024
HALF = SLOPES // 2
ROWS = 512
KEPT = 5
F32, BF16 = jnp.float32, jnp.bfloat16
SENT = BF16
PIECES = 2
WIDTH = HALF // PIECES


def parity(bits):
    for shift in (4, 2, 1):
        bits = bits ^ (bits >> shift)
    return bits & 1


def device(zh, x, y, zl, c):
    return (zh * 16 + x * 4 + y, zl * 2 + c)


BLOCKS = (((0, 0), (0, 1), (3, 1), (0, 2), (1, 2)), ((1, 0), (1, 1), (2, 0), (2, 1), (2, 2)))


GROUPS = ((0, 1), (1, 2), (2, 3), (3, 4), (4, 5))


def is_computed(dx, dy):
    return jnp.where(((dx < 3) & (dy < 3)) | ((dx == 3) & (dy == 1)), 1, 0)


def is_mirrored(dx, dy):
    return (dx % 2, dy % 2) != (0, 0)


def demodulation_kernel(
    push_ref,
    pull_ref,
    order_hbm,
    map_hbm,
    out_ref,
    push,
    pull,
    order_ref,
    map_ref,
    difference,
    total,
    transformed,
    mixed,
    row_block,
    col_block,
    relay,
    pair_out,
    pair_in,
    part,
    ring_out,
    ring_in,
    final_out,
    final_in,
    load_sem,
    table_sem,
    mix_send,
    mix_recv,
    gather_send,
    gather_recv,
    pair_send,
    pair_recv,
    ring_send,
    ring_recv,
    final_send,
    final_recv,
):
    poke, sensor = lax.axis_index("poke"), lax.axis_index("sensor")
    zh, x, y = poke // 16, (poke // 4) % 4, poke % 4
    zl, c = sensor // 2, sensor % 2
    z = zh * 4 + zl
    zz2, b = zl // 2, zl % 2

    def remote(src, dst, send, recv, target):
        return pltpu.make_async_remote_copy(
            src_ref=src, dst_ref=dst, send_sem=send, recv_sem=recv, device_id=target, device_id_type=MESH
        )

    def load(star):
        return (
            pltpu.make_async_copy(push_ref.at[star], push.at[star], load_sem.at[0, star]),
            pltpu.make_async_copy(pull_ref.at[star], pull.at[star], load_sem.at[1, star]),
        )

    tables = [
        pltpu.make_async_copy(order_hbm, order_ref, table_sem.at[0]),
        pltpu.make_async_copy(map_hbm, map_ref, table_sem.at[1]),
    ]
    for copy in tables:
        copy.start()

    def start_load(star, _):
        for copy in load(star):
            copy.start()
        return 0

    lax.fori_loop(0, STARS, start_load, 0)

    barrier = pltpu.get_barrier_semaphore()

    def greet(target):
        pl.semaphore_signal(barrier, inc=1, device_id=target, device_id_type=MESH)

    def mix_target(o):
        return (zh + 1 - o // 16) % 2, (x + (o // 4) % 4) % 4, (y + o % 4) % 4

    def greet_mix(o, _):
        zh2, x2, y2 = mix_target(o)
        greet(device(zh2, x2, y2, zl, c))
        return 0

    def greet_direct(o, _):
        greet(device(zh, x, (y + o // 4) % 4, 2 * zz2 + (b + o // 2) % 2, (c + o) % 2))
        return 0

    def greet_mirror(o, _):
        greet(device(zz2, (x + o // 4) % 4, y, 2 * zh + (b + o // 2) % 2, (c + o) % 2))
        return 0

    lax.fori_loop(0, 16, greet_mix, 0)
    lax.fori_loop(17, 32, greet_mix, 0)
    lax.fori_loop(1, 16, greet_direct, 0)
    lax.fori_loop(1, 16, greet_mirror, 0)
    for step in (1, 7):
        greet(device((z + step) % 8 // 4, x, y, (z + step) % 4, c))

    @pl.when(zz2 != zh)
    def _():
        greet(device(zz2, x, y, 2 * zh + b, c))

    for copy in tables:
        copy.wait()
    row = lax.broadcasted_iota(jnp.int32, (FRAMES, FRAMES), 0)
    mode = (row // 8 % 2) * 128 + (row // 16) * 8 + row % 8
    local_sign = (1 - 2 * parity(mode & order_ref[...])).astype(F32).astype(BF16)

    def average(half, piece, first):
        def star_step(star, _):
            if first:
                for copy in load(star):
                    copy.wait()
                difference[star] = (push[star].astype(F32) - pull[star].astype(F32)).astype(BF16)
            columns = pl.ds(pl.multiple_of(half * HALF + piece * WIDTH, 128), WIDTH)
            index = jnp.where(lax.broadcasted_iota(jnp.int32, (STARS, WIDTH), 0) == star, map_ref[:, columns], 0)
            index = jnp.sum(index, axis=0, keepdims=True) % SLOPES
            hot = (lax.broadcasted_iota(jnp.int32, (SLOPES, WIDTH), 0) == index).astype(F32).astype(BF16)
            total[...] += jnp.dot(difference[star], hot, preferred_element_type=F32)
            return 0

        total[...] = jnp.zeros_like(total)
        lax.fori_loop(0, STARS, star_step, 0)
        averaged = total[...] / STARS
        high = averaged.astype(BF16)
        low = (averaged - high.astype(F32)).astype(BF16)
        t = jnp.dot(local_sign, high, preferred_element_type=F32)
        t += jnp.dot(local_sign, low, preferred_element_type=F32)
        transformed[half, piece] = t.astype(BF16)

    def mix_copy(piece, o):
        zh2, x2, y2 = mix_target(o)
        rows = pl.multiple_of(16 * (4 * x2 + y2), 16)
        return remote(
            transformed.at[zh2, piece, pl.ds(rows, 16)],
            mixed.at[piece, pl.ds(pl.multiple_of(16 * poke, 16), 16)],
            mix_send.at[piece, o],
            mix_recv.at[piece, o],
            device(zh2, x2, y2, zl, c),
        )

    def start_mix(piece, lo, hi):
        lax.fori_loop(lo, hi, lambda o, _: (mix_copy(piece, o).start(), 0)[1], 0)

    def wait_mix(piece, lo, hi):
        lax.fori_loop(lo, hi, lambda o, _: (mix_copy(piece, o).wait(), 0)[1], 0)

    for piece in range(PIECES):
        average(1 - zh, piece, piece == 0)
        if piece == 0:
            pl.semaphore_wait(barrier, 31 + 15 + 15 + 2 + jnp.where(zz2 != zh, 1, 0))
        start_mix(piece, 0, 16)
        average(zh, piece, False)
        start_mix(piece, 17, 32)
        mixed[piece, pl.ds(pl.multiple_of(16 * poke, 16), 16), :] = transformed[
            zh, piece, pl.ds(pl.multiple_of(16 * (4 * x + y), 16), 16), :
        ]

    row = lax.broadcasted_iota(jnp.int32, (ROWS, ROWS), 0)
    col = lax.broadcasted_iota(jnp.int32, (ROWS, ROWS), 1)
    sign = 1 - 2 * parity((row % 32) & (col // 16))
    sign = jnp.where(row // 32 == col % 16, sign, 0).astype(F32).astype(BF16)

    def gather(src, dst, piece, k, dx, dy):
        target = device(zh, (x + dx) % 4, (y + dy) % 4, zl, c)
        return remote(src, dst, gather_send.at[piece, k], gather_recv.at[piece, k], target)

    low, high = pl.ds(0, ROWS // 2), pl.ds(ROWS // 2, ROWS // 2)

    def near_copies(piece):
        return [
            gather(col_block.at[0, piece], col_block.at[1, piece], piece, 0, 3, 0),
            gather(row_block.at[0, piece], row_block.at[1, piece], piece, 1, 0, 3),
            gather(col_block.at[0, piece], col_block.at[3, piece], piece, 2, 1, 0),
            gather(row_block.at[0, piece, high], relay.at[piece], piece, 3, 0, 1),
        ]

    def far_col_copies(piece):
        return [
            gather(col_block.at[1, piece, low], col_block.at[2, piece, low], piece, 4, 3, 0),
            gather(col_block.at[3, piece, high], col_block.at[2, piece, high], piece, 5, 1, 0),
        ]

    def far_row_copies(piece):
        return [
            gather(row_block.at[1, piece, low], row_block.at[2, piece, low], piece, 6, 0, 3),
            gather(relay.at[piece], row_block.at[2, piece, high], piece, 7, 0, 1),
        ]

    near, far_col, far_row = [], [], []
    for piece in range(PIECES):
        wait_mix(piece, 0, 16)
        wait_mix(piece, 17, 32)
        demodulated = jnp.dot(sign, mixed[piece], preferred_element_type=F32)
        demodulated = (demodulated * (1.0 / math.sqrt(8192))).astype(BF16)
        row_block[0, piece] = demodulated
        col_block[0, piece] = demodulated
        for copy in near_copies(piece):
            copy.start()
            near.append(copy)
    for piece in range(PIECES):
        far_col += far_col_copies(piece)
        far_row += far_row_copies(piece)

    def pick(core, tau):
        (dx0, dy0), (dx1, dy1) = BLOCKS[0][tau], BLOCKS[1][tau]
        return dx0 + core * (dx1 - dx0), dy0 + core * (dy1 - dy0)

    def block(core, tau):
        dx, dy = pick(core, tau)
        value = None
        for piece in range(PIECES):
            term = lax.dot_general(
                row_block[dy, piece],
                col_block[dx, piece],
                (((1,), (1,)), ((), ())),
                preferred_element_type=F32,
            )
            value = term if value is None else value + term
        return value

    def pair_copy(tau):
        return remote(
            pair_out.at[tau], pair_in.at[tau], pair_send.at[tau], pair_recv.at[tau], device(zh, x, y, zl, 1 - c)
        )

    def ring_copy(g, way, d, half):
        z2 = (z + (1 if way == 0 else 7)) % 8
        lo, hi = GROUPS[g]
        return remote(
            ring_out.at[way, d, half, lo:hi],
            ring_in.at[way, d, half, lo:hi],
            ring_send.at[g, way, d, half],
            ring_recv.at[g, way, d, half],
            device(z2 // 4, x, y, z2 % 4, c),
        )

    def ring_step(g, way, d, half, first=False):
        lo, hi = GROUPS[g]
        chunk = (z + (d if way == 0 else 8 - d)) % 8
        value = part[lo:hi, chunk, half * 64 : half * 64 + 64, :]
        if not first:
            ring_copy(g, way, d, half).wait_recv()
            value = value + ring_in[way, d, half, lo:hi].astype(F32)
        ring_out[way, d - 1, half, lo:hi] = value.astype(BF16)
        ring_copy(g, way, d - 1, half).start()

    def give(tau):
        pair_out[tau] = block(1 - c, tau).astype(BF16)
        pair_copy(tau).start()

    def keep(tau):
        value = block(c, tau)
        pair_copy(tau).wait_recv()
        value += pair_in[tau].astype(F32)
        for j in range(8):
            r, s = (j // 4) * 256 + (j % 2) * 128, (j // 2 % 2) * 256
            part[tau, j] = value[r : r + 128, s : s + 256]

    def begin(g):
        ring_step(g, 0, 4, 0, True)
        ring_step(g, 1, 4, 1, True)
        ring_step(g, 0, 3, 1, True)
        ring_step(g, 1, 3, 0, True)

    def progress(g, d):
        ring_step(g, 0, d, 0)
        ring_step(g, 1, d, 1)
        if d > 1:
            ring_step(g, 0, d - 1, 1)
            ring_step(g, 1, d - 1, 0)

    def is_here(target):
        return (target[0] == poke) & (target[1] == sensor)

    def ship(src, dst, send, recv, target):
        here = is_here(target)

        @pl.when(here)
        def _():
            pltpu.make_async_copy(src, dst, recv).start()

        @pl.when(jnp.logical_not(here))
        def _():
            remote(src, dst, send, recv, target).start()

    def shipped(src, dst, send, recv, target):
        @pl.when(jnp.logical_not(is_here(target)))
        def _():
            remote(src, dst, send, recv, target).wait_send()

    def direct(tau):
        dx, dy = pick(c, tau)
        i, j = (x + dx) % 4, (y + dy) % 4
        target = device(zh, x, j, 2 * zz2 + i // 2, i % 2)
        return final_out.at[0, tau], final_in.at[y, b], final_send.at[0, tau], final_recv.at[y, b], target

    def mirrored(tau):
        dx, dy = pick(c, tau)
        i, j = (x + dx) % 4, (y + dy) % 4
        target = device(zz2, i, y, 2 * zh + x // 2, x % 2)
        return final_out.at[1, tau], final_in.at[j, b], final_send.at[1, tau], final_recv.at[j, b], target

    def when_mirrored(tau, action):
        cores = [core for core in (0, 1) if is_mirrored(*BLOCKS[core][tau])]
        if len(cores) == 2:
            action()
        elif cores:
            pl.when(c == cores[0])(action)

    def finish(g):
        for way in (0, 1):
            for half in (0, 1):
                ring_copy(g, way, 0, half).wait_recv()
        for tau in range(*GROUPS[g]):
            value = part[tau, z] + ring_in[0, 0, :, tau].reshape(128, 256).astype(F32)
            value += ring_in[1, 0, :, tau].reshape(128, 256).astype(F32)
            value *= 1.0 / math.sqrt(8192)
            final_out[0, tau, 0] = value[:, :128].astype(SENT)
            final_out[0, tau, 1] = value[:, 128:].astype(SENT)
            ship(*direct(tau))

            def send_mirror(tau=tau, value=value):
                final_out[1, tau, 0] = value[:, :128].T.astype(SENT)
                final_out[1, tau, 1] = value[:, 128:].T.astype(SENT)
                ship(*mirrored(tau))

            when_mirrored(tau, send_mirror)

    for copy in near:
        copy.wait_recv()
    for copy in far_col + far_row:
        copy.start()
    give(0)
    give(1)
    keep(0)
    begin(0)
    keep(1)
    begin(1)
    for d in (3, 2):
        progress(0, d)
        progress(1, d)
    for copy in far_col:
        copy.wait_recv()
    give(2)
    progress(0, 1)
    progress(1, 1)
    keep(2)
    begin(2)
    for copy in far_row:
        copy.wait_recv()
    give(3)
    give(4)
    finish(0)
    keep(3)
    begin(3)
    finish(1)
    keep(4)
    begin(4)
    for d in (3, 2, 1):
        for g in (2, 3, 4):
            progress(g, d)
    for g in (2, 3, 4):
        finish(g)

    for j in range(4):
        direct_in = is_computed((sensor - 4 * zz2 - x + 4) % 4, (y - j + 4) % 4)
        for half in range(2):
            pltpu.make_async_copy(final_out.at[0, 0], final_in.at[j, half], final_recv.at[j, half]).wait()
            for w in range(2):
                rows = half * direct_in + w * (1 - direct_in)
                cols = w * direct_in + half * (1 - direct_in)
                out_ref[
                    pl.ds(pl.multiple_of(rows * 128, 128), 128),
                    pl.ds(pl.multiple_of(j * 256 + cols * 128, 128), 128),
                ] = final_in[j, half, w]

    for copy in near + far_col + far_row:
        copy.wait_send()
    for g in range(len(GROUPS)):
        for d in (3, 2, 1, 0):
            for way in (0, 1):
                for half in (0, 1):
                    if d < 3 or way == half:
                        ring_copy(g, way, d, half).wait_send()
    for tau in range(KEPT):
        pair_copy(tau).wait_send()
        shipped(*direct(tau))
        when_mirrored(tau, lambda tau=tau: shipped(*mirrored(tau)))


def local(push_slopes, pull_slopes, pattern_order, star_map):
    dma = pltpu.SemaphoreType.DMA
    vmem = pl.BlockSpec(memory_space=pltpu.VMEM)
    hbm = pl.BlockSpec(memory_space=pl.ANY)
    return pl.pallas_call(
        demodulation_kernel,
        out_shape=jax.ShapeDtypeStruct((256, 1024), SENT),
        in_specs=[hbm] * 4,
        out_specs=vmem,
        scratch_shapes=[
            pltpu.VMEM((STARS, FRAMES, SLOPES), BF16),
            pltpu.VMEM((STARS, FRAMES, SLOPES), BF16),
            pltpu.VMEM((1, FRAMES), jnp.int32),
            pltpu.VMEM((STARS, SLOPES), jnp.int32),
            pltpu.VMEM((STARS, FRAMES, SLOPES), BF16),
            pltpu.VMEM((FRAMES, WIDTH), F32),
            pltpu.VMEM((2, PIECES, FRAMES, WIDTH), BF16),
            pltpu.VMEM((PIECES, ROWS, WIDTH), BF16),
            pltpu.VMEM((3, PIECES, ROWS, WIDTH), BF16),
            pltpu.VMEM((4, PIECES, ROWS, WIDTH), BF16),
            pltpu.VMEM((PIECES, ROWS // 2, WIDTH), BF16),
            pltpu.VMEM((KEPT, ROWS, ROWS), BF16),
            pltpu.VMEM((KEPT, ROWS, ROWS), BF16),
            pltpu.VMEM((KEPT, 8, 128, 256), F32),
            pltpu.VMEM((2, 4, 2, KEPT, 64, 256), BF16),
            pltpu.VMEM((2, 4, 2, KEPT, 64, 256), BF16),
            pltpu.VMEM((2, KEPT, 2, 128, 128), SENT),
            pltpu.VMEM((4, 2, 2, 128, 128), SENT),
            dma((2, STARS)),
            dma((2,)),
            dma((PIECES, 32)),
            dma((PIECES, 32)),
            dma((PIECES, 8)),
            dma((PIECES, 8)),
            dma((KEPT,)),
            dma((KEPT,)),
            dma((len(GROUPS), 2, 4, 2)),
            dma((len(GROUPS), 2, 4, 2)),
            dma((2, KEPT)),
            dma((4, 2)),
        ],
        compiler_params=pltpu.CompilerParams(
            collective_id=0, has_side_effects=True, vmem_limit_bytes=56 * 2**20
        ),
        name="demodulation",
    )(
        jnp.transpose(push_slopes, (1, 0, 2)),
        jnp.transpose(pull_slopes, (1, 0, 2)),
        pattern_order.reshape(1, -1),
        star_map,
    ).astype(F32)


def solution(mesh):
    return jax.shard_map(
        local,
        mesh=mesh,
        in_specs=(P("poke", None, "sensor"), P("poke", None, "sensor"), P(), P(None, "sensor")),
        out_specs=P("poke", "sensor"),
        check_vma=False,
    )
```

```python
import functools
import math

import jax
import jax.numpy as jnp
from jax import lax
from jax.experimental import pallas as pl
from jax.experimental.pallas import tpu as pltpu
from jax.sharding import PartitionSpec as P

MESH = pl.DeviceIdType.MESH
STARS, FRAMES, SLOPES = 6, 256, 1024
HALF = SLOPES // 2
ROWS = 512
KEPT = 5
F32, BF16 = jnp.float32, jnp.bfloat16
SENT = BF16
PIECES = 2
WIDTH = HALF // PIECES


def parity(bits):
    for shift in (4, 2, 1):
        bits = bits ^ (bits >> shift)
    return bits & 1


def device(zh, x, y, zl, c):
    return (zh * 16 + x * 4 + y, zl * 2 + c)


BLOCKS = (((0, 0), (0, 1), (3, 1), (0, 2), (1, 2)), ((1, 0), (1, 1), (2, 0), (2, 1), (2, 2)))


GROUPS = ((0, 1), (1, 2), (2, 3), (3, 4), (4, 5))


def is_computed(dx, dy):
    return jnp.where(((dx < 3) & (dy < 3)) | ((dx == 3) & (dy == 1)), 1, 0)


def is_mirrored(dx, dy):
    return (dx % 2, dy % 2) != (0, 0)


def demodulation_kernel(
    push_ref,
    pull_ref,
    order_hbm,
    map_hbm,
    out_ref,
    push,
    pull,
    order_ref,
    map_ref,
    difference,
    total,
    transformed,
    mixed,
    row_block,
    col_block,
    relay,
    pair_out,
    pair_in,
    part,
    ring_out,
    ring_in,
    final_out,
    final_in,
    load_sem,
    table_sem,
    mix_send,
    mix_recv,
    gather_send,
    gather_recv,
    pair_send,
    pair_recv,
    ring_send,
    ring_recv,
    final_send,
    final_recv,
):
    poke, sensor = lax.axis_index("poke"), lax.axis_index("sensor")
    zh, x, y = poke // 16, (poke // 4) % 4, poke % 4
    zl, c = sensor // 2, sensor % 2
    z = zh * 4 + zl
    zz2, b = zl // 2, zl % 2

    def remote(src, dst, send, recv, target):
        return pltpu.make_async_remote_copy(
            src_ref=src, dst_ref=dst, send_sem=send, recv_sem=recv, device_id=target, device_id_type=MESH
        )

    def load(star):
        return (
            pltpu.make_async_copy(push_ref.at[star], push.at[star], load_sem.at[0, star]),
            pltpu.make_async_copy(pull_ref.at[star], pull.at[star], load_sem.at[1, star]),
        )

    tables = [
        pltpu.make_async_copy(order_hbm, order_ref, table_sem.at[0]),
        pltpu.make_async_copy(map_hbm, map_ref, table_sem.at[1]),
    ]
    for copy in tables:
        copy.start()

    def start_load(star, _):
        for copy in load(star):
            copy.start()
        return 0

    lax.fori_loop(0, STARS, start_load, 0)

    barrier = pltpu.get_barrier_semaphore()

    def greet(target):
        pl.semaphore_signal(barrier, inc=1, device_id=target, device_id_type=MESH)

    def mix_target(o):
        return (zh + 1 - o // 16) % 2, (x + (o // 4) % 4) % 4, (y + o % 4) % 4

    def greet_mix(o, _):
        zh2, x2, y2 = mix_target(o)
        greet(device(zh2, x2, y2, zl, c))
        return 0

    def greet_direct(o, _):
        greet(device(zh, x, (y + o // 4) % 4, 2 * zz2 + (b + o // 2) % 2, (c + o) % 2))
        return 0

    def greet_mirror(o, _):
        greet(device(zz2, (x + o // 4) % 4, y, 2 * zh + (b + o // 2) % 2, (c + o) % 2))
        return 0

    lax.fori_loop(0, 16, greet_mix, 0)
    lax.fori_loop(17, 32, greet_mix, 0)
    lax.fori_loop(1, 16, greet_direct, 0)
    lax.fori_loop(1, 16, greet_mirror, 0)
    for step in (1, 7):
        greet(device((z + step) % 8 // 4, x, y, (z + step) % 4, c))

    @pl.when(zz2 != zh)
    def _():
        greet(device(zz2, x, y, 2 * zh + b, c))

    for copy in tables:
        copy.wait()
    row = lax.broadcasted_iota(jnp.int32, (FRAMES, FRAMES), 0)
    mode = (row // 8 % 2) * 128 + (row // 16) * 8 + row % 8
    local_sign = (1 - 2 * parity(mode & order_ref[...])).astype(F32).astype(BF16)

    def average(half, piece, first):
        def star_step(star, _):
            if first:
                for copy in load(star):
                    copy.wait()
                difference[star] = (push[star].astype(F32) - pull[star].astype(F32)).astype(BF16)
            columns = pl.ds(pl.multiple_of(half * HALF + piece * WIDTH, 128), WIDTH)
            index = jnp.where(lax.broadcasted_iota(jnp.int32, (STARS, WIDTH), 0) == star, map_ref[:, columns], 0)
            index = jnp.sum(index, axis=0, keepdims=True) % SLOPES
            hot = (lax.broadcasted_iota(jnp.int32, (SLOPES, WIDTH), 0) == index).astype(F32).astype(BF16)
            total[...] += jnp.dot(difference[star], hot, preferred_element_type=F32)
            return 0

        total[...] = jnp.zeros_like(total)
        lax.fori_loop(0, STARS, star_step, 0)
        averaged = total[...] / STARS
        high = averaged.astype(BF16)
        low = (averaged - high.astype(F32)).astype(BF16)
        t = jnp.dot(local_sign, high, preferred_element_type=F32)
        t += jnp.dot(local_sign, low, preferred_element_type=F32)
        transformed[half, piece] = t.astype(BF16)

    def mix_copy(piece, o):
        zh2, x2, y2 = mix_target(o)
        rows = pl.multiple_of(16 * (4 * x2 + y2), 16)
        return remote(
            transformed.at[zh2, piece, pl.ds(rows, 16)],
            mixed.at[piece, pl.ds(pl.multiple_of(16 * poke, 16), 16)],
            mix_send.at[piece, o],
            mix_recv.at[piece, o],
            device(zh2, x2, y2, zl, c),
        )

    def start_mix(piece, lo, hi):
        lax.fori_loop(lo, hi, lambda o, _: (mix_copy(piece, o).start(), 0)[1], 0)

    def wait_mix(piece, lo, hi):
        lax.fori_loop(lo, hi, lambda o, _: (mix_copy(piece, o).wait(), 0)[1], 0)

    for piece in range(PIECES):
        average(1 - zh, piece, piece == 0)
        if piece == 0:
            pl.semaphore_wait(barrier, 31 + 15 + 15 + 2 + jnp.where(zz2 != zh, 1, 0))
        start_mix(piece, 0, 16)
        average(zh, piece, False)
        start_mix(piece, 17, 32)
        mixed[piece, pl.ds(pl.multiple_of(16 * poke, 16), 16), :] = transformed[
            zh, piece, pl.ds(pl.multiple_of(16 * (4 * x + y), 16), 16), :
        ]

    row = lax.broadcasted_iota(jnp.int32, (ROWS, ROWS), 0)
    col = lax.broadcasted_iota(jnp.int32, (ROWS, ROWS), 1)
    sign = 1 - 2 * parity((row % 32) & (col // 16))
    sign = jnp.where(row // 32 == col % 16, sign, 0).astype(F32).astype(BF16)

    def gather(src, dst, piece, k, dx, dy):
        target = device(zh, (x + dx) % 4, (y + dy) % 4, zl, c)
        return remote(src, dst, gather_send.at[piece, k], gather_recv.at[piece, k], target)

    low, high = pl.ds(0, ROWS // 2), pl.ds(ROWS // 2, ROWS // 2)

    def near_copies(piece):
        return [
            gather(col_block.at[0, piece], col_block.at[1, piece], piece, 0, 3, 0),
            gather(row_block.at[0, piece], row_block.at[1, piece], piece, 1, 0, 3),
            gather(col_block.at[0, piece], col_block.at[3, piece], piece, 2, 1, 0),
            gather(row_block.at[0, piece, high], relay.at[piece], piece, 3, 0, 1),
        ]

    def far_col_copies(piece):
        return [
            gather(col_block.at[1, piece, low], col_block.at[2, piece, low], piece, 4, 3, 0),
            gather(col_block.at[3, piece, high], col_block.at[2, piece, high], piece, 5, 1, 0),
        ]

    def far_row_copies(piece):
        return [
            gather(row_block.at[1, piece, low], row_block.at[2, piece, low], piece, 6, 0, 3),
            gather(relay.at[piece], row_block.at[2, piece, high], piece, 7, 0, 1),
        ]

    near, far_col, far_row = [], [], []
    for piece in range(PIECES):
        wait_mix(piece, 0, 16)
        wait_mix(piece, 17, 32)
        demodulated = jnp.dot(sign, mixed[piece], preferred_element_type=F32)
        demodulated = (demodulated * (1.0 / math.sqrt(8192))).astype(BF16)
        row_block[0, piece] = demodulated
        col_block[0, piece] = demodulated
        for copy in near_copies(piece):
            copy.start()
            near.append(copy)
    for piece in range(PIECES):
        far_col += far_col_copies(piece)
        far_row += far_row_copies(piece)

    def pick(core, tau):
        (dx0, dy0), (dx1, dy1) = BLOCKS[0][tau], BLOCKS[1][tau]
        return dx0 + core * (dx1 - dx0), dy0 + core * (dy1 - dy0)

    def block(core, tau):
        dx, dy = pick(core, tau)
        value = None
        for piece in range(PIECES):
            term = lax.dot_general(
                row_block[dy, piece],
                col_block[dx, piece],
                (((1,), (1,)), ((), ())),
                preferred_element_type=F32,
            )
            value = term if value is None else value + term
        return value

    def pair_copy(tau):
        return remote(
            pair_out.at[tau], pair_in.at[tau], pair_send.at[tau], pair_recv.at[tau], device(zh, x, y, zl, 1 - c)
        )

    def ring_copy(g, way, d, half):
        z2 = (z + (1 if way == 0 else 7)) % 8
        lo, hi = GROUPS[g]
        return remote(
            ring_out.at[way, d, half, lo:hi],
            ring_in.at[way, d, half, lo:hi],
            ring_send.at[g, way, d, half],
            ring_recv.at[g, way, d, half],
            device(z2 // 4, x, y, z2 % 4, c),
        )

    def ring_step(g, way, d, half, first=False):
        lo, hi = GROUPS[g]
        chunk = (z + (d if way == 0 else 8 - d)) % 8
        value = part[lo:hi, chunk, half * 64 : half * 64 + 64, :]
        if not first:
            ring_copy(g, way, d, half).wait_recv()
            value = value + ring_in[way, d, half, lo:hi].astype(F32)
        ring_out[way, d - 1, half, lo:hi] = value.astype(BF16)
        ring_copy(g, way, d - 1, half).start()

    def give(tau):
        pair_out[tau] = block(1 - c, tau).astype(BF16)
        pair_copy(tau).start()

    def keep(tau):
        value = block(c, tau)
        pair_copy(tau).wait_recv()
        value += pair_in[tau].astype(F32)
        for j in range(8):
            r, s = (j // 4) * 256 + (j % 2) * 128, (j // 2 % 2) * 256
            part[tau, j] = value[r : r + 128, s : s + 256]

    def begin(g):
        ring_step(g, 0, 4, 0, True)
        ring_step(g, 1, 4, 1, True)
        ring_step(g, 0, 3, 1, True)
        ring_step(g, 1, 3, 0, True)

    def progress(g, d):
        ring_step(g, 0, d, 0)
        ring_step(g, 1, d, 1)
        if d > 1:
            ring_step(g, 0, d - 1, 1)
            ring_step(g, 1, d - 1, 0)

    def is_here(target):
        return (target[0] == poke) & (target[1] == sensor)

    def ship(src, dst, send, recv, target):
        here = is_here(target)

        @pl.when(here)
        def _():
            pltpu.make_async_copy(src, dst, recv).start()

        @pl.when(jnp.logical_not(here))
        def _():
            remote(src, dst, send, recv, target).start()

    def shipped(src, dst, send, recv, target):
        @pl.when(jnp.logical_not(is_here(target)))
        def _():
            remote(src, dst, send, recv, target).wait_send()

    def direct(tau):
        dx, dy = pick(c, tau)
        i, j = (x + dx) % 4, (y + dy) % 4
        target = device(zh, x, j, 2 * zz2 + i // 2, i % 2)
        return final_out.at[0, tau], final_in.at[y, b], final_send.at[0, tau], final_recv.at[y, b], target

    def mirrored(tau):
        dx, dy = pick(c, tau)
        i, j = (x + dx) % 4, (y + dy) % 4
        target = device(zz2, i, y, 2 * zh + x // 2, x % 2)
        return final_out.at[1, tau], final_in.at[j, b], final_send.at[1, tau], final_recv.at[j, b], target

    def when_mirrored(tau, action):
        cores = [core for core in (0, 1) if is_mirrored(*BLOCKS[core][tau])]
        if len(cores) == 2:
            action()
        elif cores:
            pl.when(c == cores[0])(action)

    def finish(g):
        for way in (0, 1):
            for half in (0, 1):
                ring_copy(g, way, 0, half).wait_recv()
        for tau in range(*GROUPS[g]):
            value = part[tau, z] + ring_in[0, 0, :, tau].reshape(128, 256).astype(F32)
            value += ring_in[1, 0, :, tau].reshape(128, 256).astype(F32)
            value *= 1.0 / math.sqrt(8192)
            final_out[0, tau, 0] = value[:, :128].astype(SENT)
            final_out[0, tau, 1] = value[:, 128:].astype(SENT)
            ship(*direct(tau))

            def send_mirror(tau=tau, value=value):
                final_out[1, tau, 0] = value[:, :128].T.astype(SENT)
                final_out[1, tau, 1] = value[:, 128:].T.astype(SENT)
                ship(*mirrored(tau))

            when_mirrored(tau, send_mirror)

    for copy in near:
        copy.wait_recv()
    for copy in far_col + far_row:
        copy.start()
    give(0)
    give(1)
    keep(0)
    begin(0)
    keep(1)
    begin(1)
    progress(0, 3)
    progress(1, 3)
    for copy in far_col + far_row:
        copy.wait_recv()
    give(2)
    give(3)
    give(4)
    keep(2)
    begin(2)
    progress(0, 2)
    progress(1, 2)
    keep(3)
    begin(3)
    progress(0, 1)
    progress(1, 1)
    keep(4)
    begin(4)
    progress(2, 3)
    progress(3, 3)
    progress(4, 3)
    progress(2, 2)
    progress(3, 2)
    progress(4, 2)
    progress(2, 1)
    progress(3, 1)
    progress(4, 1)
    finish(0)
    finish(1)
    finish(2)
    finish(3)
    finish(4)

    for j in range(4):
        direct_in = is_computed((sensor - 4 * zz2 - x + 4) % 4, (y - j + 4) % 4)
        for half in range(2):
            pltpu.make_async_copy(final_out.at[0, 0], final_in.at[j, half], final_recv.at[j, half]).wait()
            for w in range(2):
                rows = half * direct_in + w * (1 - direct_in)
                cols = w * direct_in + half * (1 - direct_in)
                out_ref[
                    pl.ds(pl.multiple_of(rows * 128, 128), 128),
                    pl.ds(pl.multiple_of(j * 256 + cols * 128, 128), 128),
                ] = final_in[j, half, w]

    for copy in near + far_col + far_row:
        copy.wait_send()
    for g in range(len(GROUPS)):
        for d in (3, 2, 1, 0):
            for way in (0, 1):
                for half in (0, 1):
                    if d < 3 or way == half:
                        ring_copy(g, way, d, half).wait_send()
    for tau in range(KEPT):
        pair_copy(tau).wait_send()
        shipped(*direct(tau))
        when_mirrored(tau, lambda tau=tau: shipped(*mirrored(tau)))


def local(push_slopes, pull_slopes, pattern_order, star_map):
    dma = pltpu.SemaphoreType.DMA
    vmem = pl.BlockSpec(memory_space=pltpu.VMEM)
    hbm = pl.BlockSpec(memory_space=pl.ANY)
    return pl.pallas_call(
        demodulation_kernel,
        out_shape=jax.ShapeDtypeStruct((256, 1024), SENT),
        in_specs=[hbm] * 4,
        out_specs=vmem,
        scratch_shapes=[
            pltpu.VMEM((STARS, FRAMES, SLOPES), BF16),
            pltpu.VMEM((STARS, FRAMES, SLOPES), BF16),
            pltpu.VMEM((1, FRAMES), jnp.int32),
            pltpu.VMEM((STARS, SLOPES), jnp.int32),
            pltpu.VMEM((STARS, FRAMES, SLOPES), BF16),
            pltpu.VMEM((FRAMES, WIDTH), F32),
            pltpu.VMEM((2, PIECES, FRAMES, WIDTH), BF16),
            pltpu.VMEM((PIECES, ROWS, WIDTH), BF16),
            pltpu.VMEM((3, PIECES, ROWS, WIDTH), BF16),
            pltpu.VMEM((4, PIECES, ROWS, WIDTH), BF16),
            pltpu.VMEM((PIECES, ROWS // 2, WIDTH), BF16),
            pltpu.VMEM((KEPT, ROWS, ROWS), BF16),
            pltpu.VMEM((KEPT, ROWS, ROWS), BF16),
            pltpu.VMEM((KEPT, 8, 128, 256), F32),
            pltpu.VMEM((2, 4, 2, KEPT, 64, 256), BF16),
            pltpu.VMEM((2, 4, 2, KEPT, 64, 256), BF16),
            pltpu.VMEM((2, KEPT, 2, 128, 128), SENT),
            pltpu.VMEM((4, 2, 2, 128, 128), SENT),
            dma((2, STARS)),
            dma((2,)),
            dma((PIECES, 32)),
            dma((PIECES, 32)),
            dma((PIECES, 8)),
            dma((PIECES, 8)),
            dma((KEPT,)),
            dma((KEPT,)),
            dma((len(GROUPS), 2, 4, 2)),
            dma((len(GROUPS), 2, 4, 2)),
            dma((2, KEPT)),
            dma((4, 2)),
        ],
        compiler_params=pltpu.CompilerParams(
            collective_id=0, has_side_effects=True, vmem_limit_bytes=56 * 2**20
        ),
        name="demodulation",
    )(
        jnp.transpose(push_slopes, (1, 0, 2)),
        jnp.transpose(pull_slopes, (1, 0, 2)),
        pattern_order.reshape(1, -1),
        star_map,
    ).astype(F32)


def solution(mesh):
    return jax.shard_map(
        local,
        mesh=mesh,
        in_specs=(P("poke", None, "sensor"), P("poke", None, "sensor"), P(), P(None, "sensor")),
        out_specs=P("poke", "sensor"),
        check_vma=False,
    )
```
